32 devices in a mesh: seq: 32 (over z, y, x, core), head: 1.
Axes of the slice: x: 2, y: 2, z: 4, core: 2. Of those that a mesh axis runs over, the one named last changes fastest.
Arguments:
- query_feat: bfloat16 [16384, 512], P('seq', 'head'), may hold values from -6 to 6
- key_feat: bfloat16 [16384, 512], P('seq', 'head'), may hold values from -6 to 6
- values: bfloat16 [16384, 4096], P('seq', 'head'), may hold values from -6 to 6
- conv_query: float32 [3, 512], P(None, 'head'), may hold values from -3 to 3
- conv_key: float32 [3, 512], P(None, 'head'), may hold values from -3 to 3
- conv_value: float32 [3, 4096], P(None, 'head'), may hold values from -3 to 3
- norm_gain: float32 [4096], P('head'), may hold values from 0.1 to 1.9
- out_weight: bfloat16 [4096, 4096], P('head', 'seq'), may hold values from -0.09375 to 0.09375
- stream_ids: int32 [32], replicated, may hold values from 0 to 3, never falling along the last dimension, each value on 1 to 16 neighbouring positions
Outputs:
- mixed: bfloat16 [16384, 4096], P('seq', 'head')
The draws below stay inside these ranges and needn't reach their ends.
Inputs may be any that keep to these rules, and one draw needn't show every extreme that they name: `stream_ids`: stream ids never fall along the shards; each stream holds 1 to 16 consecutive shards, and one stream holds exactly 16.
All inputs are finite; a program needn't handle non-finite values.
Results may differ from the reference program's by a relative error of at most 0.018.
Values may be sent and summed in bfloat16 or wider, within the bound.
No kernel may reach another device: no remote copies, remote signals or barrier semaphores. Data moves between devices by JAX's collectives and lax.ppermute only.
A program may use at most 320 MiB of HBM per device.

```python
import math
import jax
import jax.numpy as jnp
import numpy as np
from jax import lax

D = 4096
HEADS = 32
HD = 128
FEAT = 16
TOK_DEV = 512
TAYLOR = 273
BLOCK = 512
TOKENS = 16384
SHARDS = 32
STREAMS = 4
MOST_RUN = 16
N_HEAD = 1


def block_levels(rng, extent, shards, low, largest):
    def one(axis_at, parts):
        heights = jax.random.uniform(jax.random.fold_in(jax.random.fold_in(rng, 6), axis_at), (parts,), jnp.float32, low / len(shards), largest / len(shards))
        return jnp.repeat(jnp.exp(heights), extent[axis_at] // parts).reshape((-1,) + (1,) * (len(extent) - axis_at - 1))

    level = one(*shards[0])
    for cut in shards[1:]:
        level = level * one(*cut)
    return level


def profile(number_of, total, limit, slope):
    portions = [(1 << 20) // math.isqrt(standing ** slope) + 1 for standing in range(2, number_of + 1)]
    spare, holding = total - limit - (number_of - 1), [1] * (number_of - 1)
    while spare > 0:
        candidates = [i for i in range(number_of - 1) if holding[i] < limit]
        pool, left = sum([portions[i] for i in candidates]), spare
        for i in candidates:
            extra = min(limit - holding[i], max(1, left * portions[i] // pool), spare)
            holding[i] = holding[i] + extra
            spare = spare - extra
    return np.array([limit] + holding)


def ragged_sizes(rng, number_of, total, most, skew):
    if number_of == 2:
        one = jax.random.randint(rng, (), max(1, total - most), min(most, total - 1) + 1)
        return jnp.stack([one, total - one])
    sizes = jnp.asarray(profile(number_of, total, most, skew), jnp.int32)
    pairs = (number_of - 1) // 2
    giver, taker = sizes[1:1 + 2 * pairs:2], sizes[2:2 + 2 * pairs:2]
    margin = jnp.minimum(giver - 1, most - taker)
    shifted = jax.random.randint(jax.random.fold_in(rng, 1), (pairs,), 0, 1 << 20) % (margin + 1)
    sizes = sizes.at[1:1 + 2 * pairs:2].set(giver - shifted).at[2:2 + 2 * pairs:2].set(taker + shifted)
    return sizes[jax.random.permutation(jax.random.fold_in(rng, 2), number_of)]


def gaussian(stream_key, extent, scale, reach, pieces=(), kind=jnp.bfloat16):
    array = jax.random.normal(stream_key, extent, jnp.float32) * scale
    if len(pieces) > 0:
        array = block_levels(stream_key, extent, pieces, -0.22, 0.18) * array
    return jnp.clip(array, min=-reach, max=reach).astype(kind)


def setup_inputs(seed: int = 0) -> dict:
    seeds = jax.random.split(jax.random.key(seed), 10)
    return {
        "query_feat": gaussian(seeds[0], (TOKENS, HEADS * FEAT), 1.0, 6.0, ((0, 32),)),
        "key_feat": gaussian(seeds[1], (TOKENS, HEADS * FEAT), 1.0, 6.0, ((0, 32),)),
        "values": gaussian(seeds[2], (TOKENS, HEADS * HD), 1.0, 6.0, ((0, 32),)),
        "conv_query": gaussian(seeds[3], (3, HEADS * FEAT), 0.6, 3.0, (), jnp.float32),
        "conv_key": gaussian(seeds[4], (3, HEADS * FEAT), 0.6, 3.0, (), jnp.float32),
        "conv_value": gaussian(seeds[5], (3, HEADS * HD), 0.6, 3.0, (), jnp.float32),
        "norm_gain": jnp.clip(1.0 + 0.18 * jax.random.normal(seeds[6], (HEADS * HD,), jnp.float32), 0.1, 1.9),
        "out_weight": gaussian(seeds[7], (HEADS * HD, D), (HEADS * HD) ** -0.5, 0.09375, ((1, 32),)),
        "stream_ids": jnp.searchsorted(jnp.cumsum(ragged_sizes(seeds[8], STREAMS, SHARDS, MOST_RUN, 2)), jnp.arange(SHARDS), side="right").astype(jnp.int32),
    }


def taylor(feats):
    scaled = feats * FEAT ** (-0.25)
    outer = (scaled[..., :, None] * scaled[..., None, :]).reshape(scaled.shape[:-1] + (FEAT * FEAT,)) * 0.5 ** 0.5
    ones = jnp.ones(scaled.shape[:-1] + (1,), jnp.float32)
    return jnp.concatenate([ones, scaled, outer], axis=-1)

def causal_conv(inputs, kernel, keep_one, keep_two):
    floats = inputs.astype(jnp.float32)
    width = floats.shape[1]
    prev_one = jnp.concatenate([jnp.zeros((1, width), jnp.float32), floats[:-1]], axis=0) * keep_one[:, None]
    prev_two = jnp.concatenate([jnp.zeros((2, width), jnp.float32), floats[:-2]], axis=0) * keep_two[:, None]
    return (kernel[0] * prev_two + kernel[1] * prev_one + kernel[2] * floats).astype(jnp.bfloat16)

def reference(query_feat, key_feat, values, conv_query, conv_key, conv_value, norm_gain, out_weight, stream_ids):
    tokens = query_feat.shape[0]
    shard_start = jnp.concatenate([jnp.ones((1,), jnp.float32), (stream_ids[1:] != stream_ids[:-1]).astype(jnp.float32)])
    positions = jnp.arange(tokens, dtype=jnp.int32)
    row_start = shard_start[positions // TOK_DEV]
    inner = positions % TOK_DEV
    keep_one = 1.0 - row_start * (inner < 1).astype(jnp.float32)
    keep_two = 1.0 - row_start * (inner < 2).astype(jnp.float32)
    qconv = causal_conv(query_feat, conv_query, keep_one, keep_two)
    kconv = causal_conv(key_feat, conv_key, keep_one, keep_two)
    vconv = causal_conv(values, conv_value, keep_one, keep_two)
    nblocks = tokens // BLOCK
    blocks = jnp.arange(nblocks, dtype=jnp.int32)
    first_block = (blocks * BLOCK % TOK_DEV == 0).astype(jnp.float32)
    reset = first_block * shard_start[blocks * BLOCK // TOK_DEV]
    qheads = qconv.reshape(tokens, HEADS, FEAT).transpose(1, 0, 2)
    kheads = kconv.reshape(tokens, HEADS, FEAT).transpose(1, 0, 2)
    vheads = vconv.reshape(tokens, HEADS, HD).transpose(1, 0, 2)
    gains = norm_gain.reshape(HEADS, HD)
    causal = jnp.tril(jnp.ones((BLOCK, BLOCK), jnp.float32))
    high = lax.Precision.HIGHEST

    def one_head(inputs):
        qhead, khead, vhead, gain = inputs
        phq = taylor(qhead.astype(jnp.float32)).astype(jnp.bfloat16).reshape(nblocks, BLOCK, TAYLOR).astype(jnp.float32)
        phk = taylor(khead.astype(jnp.float32)).astype(jnp.bfloat16).reshape(nblocks, BLOCK, TAYLOR).astype(jnp.float32)
        vblock = vhead.reshape(nblocks, BLOCK, HD).astype(jnp.float32)
        scores = jnp.einsum('bif,bjf->bij', phq, phk, precision=high) * causal
        scores = scores.astype(jnp.bfloat16).astype(jnp.float32)
        local = jnp.einsum('bij,bjd->bid', scores, vblock, precision=high)
        kvsum = jnp.einsum('bjf,bjd->bfd', phk, vblock, precision=high)

        def advance(carry, pair):
            block_kv, flag = pair
            entering = carry * (1.0 - flag)
            return (entering + block_kv, entering)
        _, states = lax.scan(advance, jnp.zeros((TAYLOR, HD), jnp.float32), (kvsum, reset))
        carried = jnp.einsum('bif,bfd->bid', phq, states, precision=high)
        result = (local + carried).reshape(tokens, HD)
        normed = result * lax.rsqrt(lax.optimization_barrier(jnp.mean(result * result, axis=-1, keepdims=True)) + 1e-05) * gain
        return normed.astype(jnp.bfloat16)
    hidden = lax.map(one_head, (qheads, kheads, vheads, gains))
    hidden = hidden.transpose(1, 0, 2).reshape(tokens, HEADS * HD)
    group = HEADS * HD // N_HEAD
    total = jnp.zeros((tokens, D), jnp.float32)
    for member in range(N_HEAD):
        partial_sum = jnp.dot(hidden[:, member * group:(member + 1) * group], out_weight[member * group:(member + 1) * group], preferred_element_type=jnp.float32)
        total = total + lax.optimization_barrier(partial_sum.astype(jnp.bfloat16)).astype(jnp.float32)
    return total.astype(jnp.bfloat16)
```

```python
import functools

import jax
import jax.numpy as jnp
from jax import lax
from jax.experimental import pallas as pl
from jax.experimental.pallas import tpu as pltpu
from jax.sharding import PartitionSpec as P

HD = 128
FEAT = 16
GROUP = 8
STATE = 160
BLOCK = 512
VMEM = 56 * 2**20

f32 = jnp.float32
bf16 = jnp.bfloat16


def conv(x_ref, rim_ref, w_ref, pad_ref):
    rows = x_ref.shape[0]
    pad_ref[pl.ds(8, rows), :] = x_ref[...].astype(f32)
    pad_ref[6:8, :] = rim_ref[...]
    return (
        w_ref[0:1] * pad_ref[pl.ds(6, rows), :]
        + w_ref[1:2] * pad_ref[pl.ds(7, rows), :]
        + w_ref[2:3] * pad_ref[pl.ds(8, rows), :]
    ).astype(bf16)


def state_kernel(k_ref, v_ref, rk_ref, rv_ref, ck_ref, cv_ref, kc_ref, vc_ref, kv_ref, kpad, vpad):
    kc = conv(k_ref, rk_ref, ck_ref, kpad)
    kc_ref[...] = kc
    vc_ref[...] = conv(v_ref, rv_ref, cv_ref, vpad)
    kt = (kc.astype(f32) * 0.5).T
    rows = kt.shape[1]
    place = lax.broadcasted_iota(jnp.int32, (FEAT, rows), 0)
    for h in range(GROUP):
        a = kt[FEAT * h : FEAT * (h + 1)]
        parts = [a, a * a] + [a * pltpu.roll(a, d, 0) for d in range(1, 8)]
        last = jnp.where(place >= 8, a * pltpu.roll(a, 8, 0), jnp.where(place == 0, 1.0, 0.0))
        feats = jnp.concatenate([p.astype(bf16) for p in parts + [last]], axis=0)
        kv_ref[h] = jnp.dot(
            feats, vc_ref[:, HD * h : HD * (h + 1)], preferred_element_type=f32
        ).astype(bf16)


def local_kernel(q_ref, rq_ref, cq_ref, kc_ref, vc_ref, qc_ref, loc_ref, qpad):
    qc = conv(q_ref, rq_ref, cq_ref, qpad)
    qc_ref[...] = qc
    rows = qc.shape[0]
    half = rows // 2
    head_of = lax.broadcasted_iota(jnp.int32, qc.shape, 1) // FEAT
    scaled = qc * jnp.asarray(0.25, bf16)
    keys = kc_ref[...]
    causal = lax.broadcasted_iota(jnp.int32, (half, half), 0) >= lax.broadcasted_iota(
        jnp.int32, (half, half), 1
    )
    across = (((1,), (1,)), ((), ()))

    def doubled(s):
        p = s + 1.0
        return p * p + 1.0

    for h in range(GROUP):
        own = jnp.where(head_of == h, scaled, jnp.zeros_like(scaled))
        vh = vc_ref[:, HD * h : HD * (h + 1)]
        s0 = lax.dot_general(own[:half], keys[:half], across, preferred_element_type=f32)
        s1 = lax.dot_general(own[half:], keys, across, preferred_element_type=f32)
        t0 = jnp.where(causal, doubled(s0), 0.0).astype(bf16)
        t10 = doubled(s1[:, :half]).astype(bf16)
        t11 = jnp.where(causal, doubled(s1[:, half:]), 0.0).astype(bf16)
        loc_ref[:half, HD * h : HD * (h + 1)] = 0.5 * jnp.dot(
            t0, vh[:half], preferred_element_type=f32
        )
        loc_ref[half:, HD * h : HD * (h + 1)] = 0.5 * jnp.dot(
            jnp.concatenate([t10, t11], axis=1), vh, preferred_element_type=f32
        )


def hidden_kernel(qc_ref, loc_ref, s_ref, gain_ref, out_ref, wide):
    width = GROUP * FEAT

    @pl.when(pl.program_id(0) == 0)
    def _():
        wide[...] = jnp.zeros_like(wide)

    for h in range(GROUP):
        for d in range(STATE // FEAT):
            wide[width * d + FEAT * h : width * d + FEAT * (h + 1), HD * h : HD * (h + 1)] = s_ref[
                h, FEAT * d : FEAT * (d + 1), :
            ]
    b = qc_ref[...].astype(f32) * 0.5
    place = lax.broadcasted_iota(jnp.int32, b.shape, 1) % FEAT

    def turned(d):
        return jnp.where(place >= d, pltpu.roll(b, d, 1), pltpu.roll(b, width - FEAT + d, 1))

    parts = [b, 0.5 * b * b] + [b * turned(d) for d in range(1, 8)]
    parts.append(jnp.where(place >= 8, b * turned(8), jnp.where(place == 0, 1.0, 0.0)))
    feats = jnp.concatenate([p.astype(bf16) for p in parts], axis=1)
    for h in range(0, GROUP, 2):
        pair = slice(HD * h, HD * (h + 2))
        both = loc_ref[:, pair] + jnp.dot(feats, wide[:, pair], preferred_element_type=f32)
        for e in range(2):
            y = both[:, HD * e : HD * (e + 1)]
            cols = slice(HD * (h + e), HD * (h + e + 1))
            scale = lax.rsqrt(jnp.mean(y * y, axis=-1, keepdims=True) + 1e-05)
            out_ref[:, cols] = (y * scale * gain_ref[:, cols]).astype(bf16)


def params():
    return pltpu.CompilerParams(dimension_semantics=("arbitrary",), vmem_limit_bytes=VMEM)


def flip(x, axis, bit):
    return lax.ppermute(x, axis, [(i, i ^ bit) for i in range(lax.axis_size(axis))])


def after(x, axis, distance):
    n = lax.axis_size(axis)
    return lax.ppermute(x, axis, [(i, i + distance) for i in range(n - distance)])


def entering(kv, ids, axis):
    n, me = lax.axis_size(axis), lax.axis_index(axis)
    half = kv.shape[0] // 2
    core = me % 2
    plane = me - me % 8

    def eq(i, j):
        return (ids[i] == ids[j]).astype(f32)

    first = me - core
    mine = lax.dynamic_slice_in_dim(kv, core * half, half, 0)
    theirs = lax.dynamic_slice_in_dim(kv, (1 - core) * half, half, 0)
    got = flip(theirs, axis, 1)
    kv0 = jnp.where(core == 0, mine, got).astype(f32)
    kv1 = jnp.where(core == 0, got, mine).astype(f32)
    joined = eq(first, first + 1)
    total = (kv1 + joined * kv0).astype(bf16)
    arrived = []
    for bit in (2, 4):
        upper = (me // bit) % 2
        base = me - me % (2 * bit)
        lower_last, upper_last = base + bit - 1, base + 2 * bit - 1
        link = eq(lower_last, upper_last)
        got = flip(total, axis, bit)
        arrived.append((upper * eq(lower_last, first), got))
        total = (
            jnp.where(upper == 1, 1.0, link) * total.astype(f32)
            + jnp.where(upper == 1, link, 1.0) * got.astype(f32)
        ).astype(bf16)
    back = -(-(n // 2 - 1) // 8)
    for step in range(back):
        total = after(total, axis, 8)
        source = plane - 8 * step - 1
        arrived.append(
            ((source >= 0) * eq(jnp.maximum(source, 0), first), total)
        )
    s0 = sum(weight * piece.astype(f32) for weight, piece in arrived)
    s1 = joined * (s0 + kv0)
    keep = jnp.where(core == 0, s0, s1).astype(bf16)
    send = jnp.where(core == 0, s1, s0).astype(bf16)
    got = flip(send, axis, 1)
    low = jnp.where(core == 0, keep, got)
    high = jnp.where(core == 0, got, keep)
    return jnp.concatenate([low, high], axis=0)


def padded(x, width):
    return x if x.shape[-1] == width else jnp.pad(x, ((0, 0), (0, width - x.shape[-1])))


def on_device(
    query_feat,
    key_feat,
    values,
    conv_query,
    conv_key,
    conv_value,
    norm_gain,
    out_weight,
    stream_ids,
):
    rows = query_feat.shape[0]
    width = values.shape[1]
    real = width // HD
    heads = -(-real // GROUP) * GROUP
    groups = heads // GROUP
    fw, vw = GROUP * FEAT, GROUP * HD
    weight = lax.all_gather(out_weight, "seq", axis=1, tiled=True)
    me = lax.axis_index("seq")
    start = jnp.logical_or(me == 0, stream_ids[me] != stream_ids[jnp.maximum(me - 1, 0)])
    keep = 1.0 - start.astype(f32)
    q, k = padded(query_feat, heads * FEAT), padded(key_feat, heads * FEAT)
    v = padded(values, heads * HD)
    cq, ck = padded(conv_query, heads * FEAT), padded(conv_key, heads * FEAT)
    cv = padded(conv_value, heads * HD)
    gain = padded(norm_gain[None], heads * HD)
    rim = after(jnp.concatenate([v[-2:], q[-2:], k[-2:]], axis=1), "seq", 1).astype(f32) * keep

    def cols(n, wide, offset=0):
        return pl.BlockSpec((n, wide), lambda g: (0, offset + g))

    kc, vc, kv = pl.pallas_call(
        state_kernel,
        grid=(groups,),
        in_specs=[
            cols(rows, fw),
            cols(rows, vw),
            cols(2, fw, heads + groups),
            cols(2, vw),
            cols(3, fw),
            cols(3, vw),
        ],
        out_specs=[
            cols(rows, fw),
            cols(rows, vw),
            pl.BlockSpec((GROUP, STATE, HD), lambda g: (g, 0, 0)),
        ],
        out_shape=[
            jax.ShapeDtypeStruct((rows, heads * FEAT), bf16),
            jax.ShapeDtypeStruct((rows, heads * HD), bf16),
            jax.ShapeDtypeStruct((heads, STATE, HD), bf16),
        ],
        scratch_shapes=[pltpu.VMEM((rows + 8, fw), f32), pltpu.VMEM((rows + 8, vw), f32)],
        compiler_params=params(),
        cost_estimate=pl.CostEstimate(
            flops=2 * heads * STATE * rows * HD, bytes_accessed=10 * 2**20, transcendentals=0
        ),
    )(k, v, rim, rim, ck, cv)
    qc, local = pl.pallas_call(
        local_kernel,
        grid=(groups,),
        in_specs=[
            cols(rows, fw),
            cols(2, fw, heads),
            cols(3, fw),
            cols(rows, fw),
            cols(rows, vw),
        ],
        out_specs=[cols(rows, fw), cols(rows, vw)],
        out_shape=[
            jax.ShapeDtypeStruct((rows, heads * FEAT), bf16),
            jax.ShapeDtypeStruct((rows, heads * HD), f32),
        ],
        scratch_shapes=[pltpu.VMEM((rows + 8, fw), f32)],
        compiler_params=params(),
        cost_estimate=pl.CostEstimate(
            flops=2 * heads * rows * rows * 256, bytes_accessed=14 * 2**20, transcendentals=0
        ),
    )(q, rim, cq, kc, vc)
    state = entering(kv, stream_ids, "seq")
    hidden = pl.pallas_call(
        hidden_kernel,
        grid=(groups,),
        in_specs=[
            cols(rows, fw),
            cols(rows, vw),
            pl.BlockSpec((GROUP, STATE, HD), lambda g: (g, 0, 0)),
            cols(1, vw),
        ],
        out_specs=cols(rows, vw),
        out_shape=jax.ShapeDtypeStruct((rows, heads * HD), bf16),
        scratch_shapes=[pltpu.VMEM((STATE * GROUP, vw), bf16)],
        compiler_params=params(),
        cost_estimate=pl.CostEstimate(
            flops=2 * heads * rows * 1280 * HD, bytes_accessed=14 * 2**20, transcendentals=0
        ),
    )(qc, local, state, gain)
    terms = jnp.dot(hidden[:, :width], weight, preferred_element_type=f32)
    return lax.psum_scatter(terms.astype(bf16), "head", scatter_dimension=1, tiled=True)


def solution(mesh):
    placed = (
        P("seq", "head"),
        P("seq", "head"),
        P("seq", "head"),
        P(None, "head"),
        P(None, "head"),
        P(None, "head"),
        P("head"),
        P("head", "seq"),
        P(),
    )
    return jax.shard_map(
        on_device, mesh=mesh, in_specs=placed, out_specs=P("seq", "head"), check_vma=False
    )
```

```python
import functools

import jax
import jax.numpy as jnp
from jax import lax
from jax.experimental import pallas as pl
from jax.experimental.pallas import tpu as pltpu
from jax.sharding import PartitionSpec as P

HD = 128
FEAT = 16
GROUP = 8
STATE = 160
BLOCK = 512
VMEM = 56 * 2**20

f32 = jnp.float32
bf16 = jnp.bfloat16


def conv(x_ref, rim_ref, w_ref, pad_ref):
    rows = x_ref.shape[0]
    pad_ref[pl.ds(8, rows), :] = x_ref[...].astype(f32)
    pad_ref[6:8, :] = rim_ref[...]
    return (
        w_ref[0:1] * pad_ref[pl.ds(6, rows), :]
        + w_ref[1:2] * pad_ref[pl.ds(7, rows), :]
        + w_ref[2:3] * pad_ref[pl.ds(8, rows), :]
    ).astype(bf16)


def state_kernel(start_ref, k_ref, v_ref, rk_ref, rv_ref, ck_ref, cv_ref, *refs):
    kc_ref, vc_ref, kv_ref, kpad, vpad = refs[-5:]
    kc = conv(k_ref, rk_ref, ck_ref, kpad)
    kc_ref[...] = kc
    vc_ref[...] = conv(v_ref, rv_ref, cv_ref, vpad)
    kt = (kc.astype(f32) * 0.5).T
    rows = kt.shape[1]
    place = lax.broadcasted_iota(jnp.int32, (FEAT, rows), 0)
    for h in range(GROUP):
        a = kt[FEAT * h : FEAT * (h + 1)]
        parts = [a, a * a] + [a * pltpu.roll(a, d, 0) for d in range(1, 8)]
        last = jnp.where(place >= 8, a * pltpu.roll(a, 8, 0), jnp.where(place == 0, 1.0, 0.0))
        feats = jnp.concatenate([p.astype(bf16) for p in parts + [last]], axis=0)
        kv_ref[h] = jnp.dot(
            feats, vc_ref[:, HD * h : HD * (h + 1)], preferred_element_type=f32
        ).astype(bf16)


def local_kernel(q_ref, rq_ref, cq_ref, kc_ref, vc_ref, *refs):
    qc_ref, loc_ref, qpad = refs[-3:]
    qc = conv(q_ref, rq_ref, cq_ref, qpad)
    qc_ref[...] = qc
    rows = qc.shape[0]
    half = rows // 2
    head_of = lax.broadcasted_iota(jnp.int32, qc.shape, 1) // FEAT
    scaled = qc * jnp.asarray(0.25, bf16)
    keys = kc_ref[...]
    causal = lax.broadcasted_iota(jnp.int32, (half, half), 0) >= lax.broadcasted_iota(
        jnp.int32, (half, half), 1
    )
    across = (((1,), (1,)), ((), ()))

    def doubled(s):
        p = s + 1.0
        return p * p + 1.0

    for h in range(GROUP):
        own = jnp.where(head_of == h, scaled, jnp.zeros_like(scaled))
        vh = vc_ref[:, HD * h : HD * (h + 1)]
        s0 = lax.dot_general(own[:half], keys[:half], across, preferred_element_type=f32)
        s1 = lax.dot_general(own[half:], keys, across, preferred_element_type=f32)
        t0 = jnp.where(causal, doubled(s0), 0.0).astype(bf16)
        t10 = doubled(s1[:, :half]).astype(bf16)
        t11 = jnp.where(causal, doubled(s1[:, half:]), 0.0).astype(bf16)
        loc_ref[:half, HD * h : HD * (h + 1)] = 0.5 * jnp.dot(
            t0, vh[:half], preferred_element_type=f32
        )
        loc_ref[half:, HD * h : HD * (h + 1)] = 0.5 * jnp.dot(
            jnp.concatenate([t10, t11], axis=1), vh, preferred_element_type=f32
        )


def hidden_kernel(start_ref, qc_ref, loc_ref, s_ref, gain_ref, out_ref, wide):
    width = GROUP * FEAT

    @pl.when(pl.program_id(0) == 0)
    def _():
        wide[...] = jnp.zeros_like(wide)

    for h in range(GROUP):
        for d in range(STATE // FEAT):
            wide[width * d + FEAT * h : width * d + FEAT * (h + 1), HD * h : HD * (h + 1)] = s_ref[
                h, FEAT * d : FEAT * (d + 1), :
            ]
    b = qc_ref[...].astype(f32) * 0.5
    place = lax.broadcasted_iota(jnp.int32, b.shape, 1) % FEAT

    def turned(d):
        return jnp.where(place >= d, pltpu.roll(b, d, 1), pltpu.roll(b, width - FEAT + d, 1))

    parts = [b, 0.5 * b * b] + [b * turned(d) for d in range(1, 8)]
    parts.append(jnp.where(place >= 8, b * turned(8), jnp.where(place == 0, 1.0, 0.0)))
    feats = jnp.concatenate([p.astype(bf16) for p in parts], axis=1)
    for h in range(0, GROUP, 2):
        pair = slice(HD * h, HD * (h + 2))
        both = loc_ref[:, pair] + jnp.dot(feats, wide[:, pair], preferred_element_type=f32)
        for e in range(2):
            y = both[:, HD * e : HD * (e + 1)]
            cols = slice(HD * (h + e), HD * (h + e + 1))
            scale = lax.rsqrt(jnp.mean(y * y, axis=-1, keepdims=True) + 1e-05)
            out_ref[:, cols] = (y * scale * gain_ref[:, cols]).astype(bf16)


def project_kernel(pieces, own, far, first_ref, place_ref, *refs):
    sides = own + far
    hidden, weights = refs[: 2 * sides], refs[2 * sides : 2 * sides + pieces]
    rows_in, held, done, hid_sems, sems, out_sems = refs[-6:]
    outs = refs[-6 - sides : -6]
    depth = hidden[0].shape[1]
    loads = []
    for p in range(2 * sides):
        turned = p + (0 if own and p < 2 else 1)
        at = pl.multiple_of((first_ref[0] + turned) % 2 * depth, depth)
        loads.append(
            pltpu.make_async_copy(
                hidden[p], rows_in.at[p // 2, :, pl.ds(at, depth)], hid_sems.at[p]
            )
        )
    copies = [
        pltpu.make_async_copy(weights[i], held.at[:, HD * i : HD * (i + 1)], sems.at[i])
        for i in range(pieces)
    ]
    groups = [range(c, min(c + 4, pieces)) for c in range(0, pieces, 4)]
    for copy in loads[:2] + copies[:4] + loads[2:] + copies[4:8]:
        copy.start()
    for copy in loads[:2]:
        copy.wait()
    stores = []
    for at, group in enumerate(groups):
        for copy in copies[4 * at : 4 * (at + 1)]:
            copy.wait()
        for copy in copies[4 * (at + 2) : 4 * (at + 3)]:
            copy.start()
        cols = slice(HD * group[0], HD * (group[-1] + 1))
        if own:
            mine = jnp.dot(rows_in[0], held[:, cols], preferred_element_type=f32).astype(bf16)
            for j, i in enumerate(group):
                done[i] = mine[:, HD * j : HD * (j + 1)]
                where = pl.multiple_of(place_ref[i] * HD, HD)
                store = pltpu.make_async_copy(
                    done.at[i], outs[0].at[:, pl.ds(where, HD)], out_sems.at[i]
                )
                store.start()
                stores.append(store)
        if at == 0:
            for copy in loads[2:]:
                copy.wait()
        if far:
            theirs = jnp.dot(rows_in[sides - 1], held[:, cols], preferred_element_type=f32)
            for j, i in enumerate(group):
                outs[-1][i] = theirs[:, HD * j : HD * (j + 1)].astype(bf16)
    for store in stores:
        store.wait()


def project(own, far, first, width, pieces, places, before=()):
    rows, half = (own + far)[0].shape
    count, depth = len(pieces), pieces[0].shape[0]
    smem, vmem, anywhere = (pl.BlockSpec(memory_space=m) for m in (pltpu.SMEM, pltpu.VMEM, pl.ANY))
    sides = [bool(own), bool(far)]
    outs = [
        (anywhere, jax.ShapeDtypeStruct((rows, width), bf16)),
        (vmem, jax.ShapeDtypeStruct((count, rows, HD), bf16)),
    ]
    outs = [o for o, wanted in zip(outs, sides) if wanted]
    return pl.pallas_call(
        functools.partial(project_kernel, count, *sides),
        in_specs=[smem] * 2 + [anywhere] * (2 * sum(sides) + count + len(before)),
        out_specs=[o[0] for o in outs],
        out_shape=[o[1] for o in outs],
        scratch_shapes=[
            pltpu.VMEM((sum(sides), rows, 2 * half), bf16),
            pltpu.VMEM((depth, HD * count), bf16),
            pltpu.VMEM((count, rows, HD), bf16),
            pltpu.SemaphoreType.DMA((4,)),
            pltpu.SemaphoreType.DMA((count,)),
            pltpu.SemaphoreType.DMA((count,)),
        ],
        input_output_aliases={2 + 2 * sum(sides) + count: 0} if before else {},
        compiler_params=pltpu.CompilerParams(vmem_limit_bytes=VMEM),
        cost_estimate=cost(count),
    )(first, places, *own, *far, *pieces, *before)


def place_kernel(counts, place_ref, *refs):
    blocks, out_ref, sems = refs[: len(counts)], refs[-2], refs[-1]
    copies = []
    for ref, count in zip(blocks, counts):
        for i in range(count):
            at = len(copies)
            where = pl.multiple_of(place_ref[at] * HD, HD)
            copy = pltpu.make_async_copy(ref.at[i], out_ref.at[:, pl.ds(where, HD)], sems.at[at])
            copy.start()
            copies.append(copy)
    for copy in copies:
        copy.wait()


def place(blocks, places, out):
    counts = [b.shape[0] for b in blocks]
    smem, vmem, anywhere = (pl.BlockSpec(memory_space=m) for m in (pltpu.SMEM, pltpu.VMEM, pl.ANY))
    return pl.pallas_call(
        functools.partial(place_kernel, counts),
        in_specs=[smem] + [vmem] * len(blocks) + [anywhere],
        out_specs=anywhere,
        out_shape=jax.ShapeDtypeStruct(out.shape, bf16),
        scratch_shapes=[pltpu.SemaphoreType.DMA((sum(counts),))],
        input_output_aliases={1 + len(blocks): 0},
        compiler_params=pltpu.CompilerParams(vmem_limit_bytes=VMEM),
        cost_estimate=cost(3),
    )(places, *blocks, out)


def ring(n):
    order = list(range(n))
    return order[:1] + order[1::2] + order[2::2][::-1]


def turn(x, axis):
    order = ring(lax.axis_size(axis) // 8)
    route = []
    for at, plane in enumerate(order):
        onto = order[(at + 1) % len(order)]
        route += [(plane * 8 + i, onto * 8 + i) for i in range(8)]
    return lax.ppermute(x, axis, route)


def flip(x, axis, bit):
    return lax.ppermute(x, axis, [(i, i ^ bit) for i in range(lax.axis_size(axis))])


def after(x, axis, distance):
    n = lax.axis_size(axis)
    return lax.ppermute(x, axis, [(i, i + distance) for i in range(n - distance)])


def tie(x, *others):
    return lax.optimization_barrier((x, *others))[0]


def cost(micros):
    return pl.CostEstimate(flops=micros * 2 * 10**10, bytes_accessed=2**20, transcendentals=0)


def params():
    return pltpu.CompilerParams(dimension_semantics=("arbitrary",), vmem_limit_bytes=VMEM)


class Scan:
    def __init__(self, ids, axis):
        self.ids, self.axis = ids, axis
        self.n, self.me = lax.axis_size(axis), lax.axis_index(axis)
        self.core = self.me % 2
        self.first = self.me - self.core
        self.plane = self.me - self.me % 8
        self.sums = 0.0

    def eq(self, i, j):
        return (self.ids[i] == self.ids[j]).astype(f32)

    def chip(self, mine, got):
        self.kv0 = jnp.where(self.core == 0, mine, got)
        kv1 = jnp.where(self.core == 0, got, mine)
        self.joined = self.eq(self.first, self.first + 1)
        self.total = (kv1.astype(f32) + self.joined * self.kv0.astype(f32)).astype(bf16)

    def hop(self, bit):
        return flip(self.total, self.axis, bit)

    def merge(self, bit, got):
        upper = (self.me // bit) % 2
        base = self.me - self.me % (2 * bit)
        lower_last, upper_last = base + bit - 1, base + 2 * bit - 1
        link = self.eq(lower_last, upper_last)
        got = got.astype(f32)
        self.sums = self.sums + upper * self.eq(lower_last, self.first) * got
        self.total = (
            jnp.where(upper == 1, 1.0, link) * self.total.astype(f32)
            + jnp.where(upper == 1, link, 1.0) * got
        ).astype(bf16)

    def climbs(self):
        return -(-(self.n // 2 - 1) // 8)

    def cut(self):
        part = self.total.shape[0] // 4
        spot = self.me // 2 % 4
        self.total = lax.dynamic_slice_in_dim(self.total, spot * part, part, 0)
        self.below = 0.0

    def climb(self, step):
        self.total = after(self.total, self.axis, 8)
        source = self.plane - 8 * step - 1
        same = (source >= 0) * self.eq(jnp.maximum(source, 0), self.plane)
        self.below = self.below + same * self.total.astype(f32)
        return self.total

    def gather_hop(self, bit):
        self.below = self.below.astype(bf16)
        return flip(self.below, self.axis, bit)

    def gather(self, bit, got):
        below = self.below
        upper = (self.me // bit) % 2 == 1
        self.below = jnp.concatenate(
            [jnp.where(upper, got, below), jnp.where(upper, below, got)], axis=0
        )

    def finish(self):
        s0 = self.sums + self.eq(self.plane, self.first) * self.below.astype(f32)
        s1 = self.joined * (s0 + self.kv0.astype(f32))
        keep = jnp.where(self.core == 0, s0, s1).astype(bf16)
        send = jnp.where(self.core == 0, s1, s0).astype(bf16)
        return keep, flip(send, self.axis, 1)


def padded(x, width):
    return x if x.shape[-1] == width else jnp.pad(x, ((0, 0), (0, width - x.shape[-1])))


def state_call(start, groups, k, v, rim, ck, cv, before=()):
    rows, heads = v.shape[0], v.shape[1] // HD
    fw, vw = GROUP * FEAT, GROUP * HD

    def cols(n, wide, offset=0):
        return pl.BlockSpec((n, wide), lambda g, s: (0, offset + s[0] + g))

    return pl.pallas_call(
        state_kernel,
        grid_spec=pltpu.PrefetchScalarGridSpec(
            num_scalar_prefetch=1,
            grid=(groups,),
            in_specs=[
                cols(rows, fw),
                cols(rows, vw),
                cols(2, fw, heads + heads // GROUP),
                cols(2, vw),
                cols(3, fw),
                cols(3, vw),
            ]
            + [pl.BlockSpec(memory_space=pl.ANY)] * len(before),
            out_specs=[
                cols(rows, fw),
                cols(rows, vw),
                pl.BlockSpec((GROUP, STATE, HD), lambda g, s: (g, 0, 0)),
            ],
            scratch_shapes=[pltpu.VMEM((rows + 8, fw), f32), pltpu.VMEM((rows + 8, vw), f32)],
        ),
        out_shape=[
            jax.ShapeDtypeStruct((rows, heads * FEAT), bf16),
            jax.ShapeDtypeStruct((rows, heads * HD), bf16),
            jax.ShapeDtypeStruct((groups * GROUP, STATE, HD), bf16),
        ],
        input_output_aliases={7 + i: i for i in range(len(before))},
        compiler_params=params(),
        cost_estimate=cost(3 * groups),
    )(start, k, v, rim, rim, ck, cv, *before)


def local_call(q, rim, cq, kc, vc, start, groups, before=()):
    rows, heads = vc.shape[0], vc.shape[1] // HD
    fw, vw = GROUP * FEAT, GROUP * HD

    def cols(n, wide, offset=0):
        return pl.BlockSpec((n, wide), lambda g: (0, offset + g))

    return pl.pallas_call(
        local_kernel,
        grid=(groups,),
        in_specs=[
            cols(rows, fw, start),
            cols(2, fw, heads + start),
            cols(3, fw, start),
            cols(rows, fw, start),
            cols(rows, vw, start),
        ]
        + [pl.BlockSpec(memory_space=pl.ANY)] * len(before),
        out_specs=[cols(rows, fw, start), cols(rows, vw, start)],
        out_shape=[
            jax.ShapeDtypeStruct((rows, heads * FEAT), bf16),
            jax.ShapeDtypeStruct((rows, heads * HD), f32),
        ],
        scratch_shapes=[pltpu.VMEM((rows + 8, fw), f32)],
        input_output_aliases={5 + i: i for i in range(len(before))},
        compiler_params=params(),
        cost_estimate=cost(3 * groups),
    )(q, rim, cq, kc, vc, *before)


def hidden_call(start, qc, local, state, gain):
    rows, fw, vw = qc.shape[0], GROUP * FEAT, GROUP * HD
    groups = state.shape[0] // GROUP

    def cols(n, wide):
        return pl.BlockSpec((n, wide), lambda g, s: (0, s[0] + g))

    return pl.pallas_call(
        hidden_kernel,
        grid_spec=pltpu.PrefetchScalarGridSpec(
            num_scalar_prefetch=1,
            grid=(groups,),
            in_specs=[
                cols(rows, fw),
                cols(rows, vw),
                pl.BlockSpec((GROUP, STATE, HD), lambda g, s: (g, 0, 0)),
                cols(1, vw),
            ],
            out_specs=pl.BlockSpec((rows, vw), lambda g, s: (0, g)),
            scratch_shapes=[pltpu.VMEM((STATE * GROUP, vw), bf16)],
        ),
        out_shape=jax.ShapeDtypeStruct((rows, groups * vw), bf16),
        compiler_params=params(),
        cost_estimate=cost(4 * groups),
    )(start, qc, local, state, gain)


def by_gather(q, k, v, cq, ck, cv, gain, rim, weight, ids, width):
    weight = lax.all_gather(weight, "seq", axis=1, tiled=True)
    groups = v.shape[1] // (GROUP * HD)
    zero = jnp.zeros((1,), jnp.int32)
    kc, vc, kv = state_call(zero, groups, k, v, rim, ck, cv)
    qc, local = local_call(q, rim, cq, kc, vc, 0, groups)
    scan = Scan(ids, "seq")
    half = kv.shape[0] // 2
    mine = lax.dynamic_slice_in_dim(kv, scan.core * half, half, 0)
    theirs = lax.dynamic_slice_in_dim(kv, (1 - scan.core) * half, half, 0)
    scan.chip(mine, flip(theirs, "seq", 1))
    for bit in (2, 4):
        scan.merge(bit, scan.hop(bit))
    scan.cut()
    for step in range(scan.climbs()):
        scan.climb(step)
    for bit in (2, 4):
        scan.gather(bit, scan.gather_hop(bit))
    keep, got = scan.finish()
    low = jnp.where(scan.core == 0, keep, got)
    high = jnp.where(scan.core == 0, got, keep)
    state = jnp.concatenate([low, high], axis=0)
    hidden = hidden_call(zero, qc, local, state, gain)
    return jnp.dot(hidden[:, :width], weight, preferred_element_type=f32).astype(bf16)


def by_tree(q, k, v, cq, ck, cv, gain, rim, weight, ids):
    axis = "seq"
    n, me = lax.axis_size(axis), lax.axis_index(axis)
    core = jnp.reshape(me % 2, (1,)).astype(jnp.int32)
    half = v.shape[1] // (GROUP * HD) // 2
    ties = lax.optimization_barrier

    def over_x(piece):
        return flip(piece, axis, 2)

    def over_y(piece):
        return flip(piece, axis, 4)

    def over_z(piece):
        return turn(piece, axis)

    def share(piece):
        return flip(piece, axis, 1)

    own0, width = weight, n * weight.shape[1]
    scan = Scan(ids, axis)
    *kept, theirs = state_call((1 - core) * half, half, k, v, rim, ck, cv)
    got = share(theirs)
    x0, y0, own1 = over_x(own0), over_y(own0), over_z(own0)
    kc, vc, mine = state_call(core * half, half, k, v, rim, ck, cv, kept)
    got = tie(got, mine)
    scan.chip(mine, got)
    hop_x = scan.hop(2)
    before = local_call(tie(q, scan.total), rim, cq, kc, vc, 0, half)
    y0, own1 = ties((y0, own1, before[1]))[:2]

    own2, d0 = over_z(own1), over_x(y0)
    hop_x, x0 = ties((hop_x, x0, before[1]))[:2]
    scan.merge(2, hop_x)
    hop_y = scan.hop(4)
    qc, local = local_call(tie(q, scan.total), rim, cq, kc, vc, half, half, before)
    y1 = over_y(tie(own1, local))
    hop_y = tie(hop_y, local)
    scan.merge(4, hop_y)
    scan.cut()

    for step in range(scan.climbs()):
        hop_z = scan.climb(step)
    scan.below, own2 = ties((scan.below, own2))
    own3 = over_z(tie(own2, scan.below))
    hop_x = scan.gather_hop(2)
    hop_x, d0 = ties((hop_x, d0))
    x1 = over_x(tie(own1, hop_x))
    scan.gather(2, hop_x)
    hop_y = scan.gather_hop(4)
    hop_y, y1 = ties((hop_y, y1))
    y2 = over_y(tie(own2, hop_y))
    d1 = over_z(tie(d0, hop_y))
    scan.gather(4, hop_y)
    keep, got = scan.finish()
    keep, own3 = ties((keep, own3))
    x3 = over_x(own3)
    hid_a = hidden_call(core * half, qc, local, keep, gain)
    got, x1 = ties((got, x1, hid_a))[:2]
    y3 = over_y(tie(own3, got))
    far_a = share(hid_a)
    hid_b = hidden_call((1 - core) * half, qc, local, got, gain)
    far_a, d1, y2 = ties((far_a, d1, y2, hid_b))[:3]
    d2, x2 = over_z(d1), over_x(tie(own2, y2))
    far_b = share(hid_b)
    soon = [
        (own0, 0, 0), (own1, 1, 0), (own2, 2, 0), (own3, 3, 0), (y0, 0, 4), (y1, 1, 4),
        (y2, 2, 4), (x0, 0, 2), (x1, 1, 2), (d0, 0, 6), (d1, 1, 6),
    ]
    late = [(None, 3, 4), (None, 3, 2), (None, 2, 6), (None, 2, 2), (None, 3, 6)]
    order = ring(n // 8)
    home = jnp.asarray(order, jnp.int32)
    spot = jnp.asarray([order.index(p) for p in range(n // 8)], jnp.int32)[me // 8]
    shift = jnp.asarray([p[1] for p in soon + late], jnp.int32)
    bits = jnp.asarray([p[2] for p in soon + late], jnp.int32)
    places = (home[(spot - shift) % (n // 8)] * 8 + (me % 8 ^ bits)).astype(jnp.int32)
    pieces, early = [p[0] for p in soon], places[: len(soon)]
    (out,) = project((hid_a, hid_b), (), core, width, pieces, early)
    far_b, x3, y3, d2, out = ties((far_b, x3, y3, d2, out))
    mid = x3.shape[0] // 2
    d3y, d3z = over_y(x3[:mid]), over_z(d2[mid:])
    (back_a,) = project((), (far_a, far_b), core, width, pieces, early)
    d3y, d3z, x2, out = ties((d3y, d3z, x2, out, back_a))[:4]
    pieces = [y3, x3, d2, x2, jnp.concatenate([d3y, d3z], axis=0)]
    out, back_b = project(
        (hid_a, hid_b), (far_a, far_b), core, width, pieces, places[len(soon) :], (out,)
    )
    back_a, back_b = share(back_a), share(back_b)
    return place([back_a, back_b], places ^ 1, out)


def on_device(
    query_feat,
    key_feat,
    values,
    conv_query,
    conv_key,
    conv_value,
    norm_gain,
    out_weight,
    stream_ids,
):
    width = values.shape[1]
    heads = -(-width // (HD * GROUP)) * GROUP
    me = lax.axis_index("seq")
    start = jnp.logical_or(me == 0, stream_ids[me] != stream_ids[jnp.maximum(me - 1, 0)])
    keep = 1.0 - start.astype(f32)
    q, k = padded(query_feat, heads * FEAT), padded(key_feat, heads * FEAT)
    v = padded(values, heads * HD)
    cq, ck = padded(conv_query, heads * FEAT), padded(conv_key, heads * FEAT)
    cv = padded(conv_value, heads * HD)
    gain = padded(norm_gain[None], heads * HD)
    rim = after(jnp.concatenate([v[-2:], q[-2:], k[-2:]], axis=1), "seq", 1).astype(f32) * keep
    n, cut = lax.axis_size("seq"), lax.axis_size("head")
    if n == 32 and cut == 1 and out_weight.shape[1] == HD and heads % (2 * GROUP) == 0:
        return by_tree(q, k, v, cq, ck, cv, gain, rim, out_weight, stream_ids)
    terms = by_gather(q, k, v, cq, ck, cv, gain, rim, out_weight, stream_ids, width)
    return lax.psum_scatter(terms, "head", scatter_dimension=1, tiled=True)


def solution(mesh):
    placed = (
        P("seq", "head"),
        P("seq", "head"),
        P("seq", "head"),
        P(None, "head"),
        P(None, "head"),
        P(None, "head"),
        P("head"),
        P("head", "seq"),
        P(),
    )
    return jax.shard_map(
        on_device, mesh=mesh, in_specs=placed, out_specs=P("seq", "head"), check_vma=False
    )
```

```python
import functools

import jax
import jax.numpy as jnp
from jax import lax
from jax.experimental import pallas as pl
from jax.experimental.pallas import tpu as pltpu
from jax.sharding import PartitionSpec as P

HD = 128
FEAT = 16
GROUP = 8
STATE = 160
BLOCK = 512
VMEM = 56 * 2**20

f32 = jnp.float32
bf16 = jnp.bfloat16


def conv(x_ref, rim_ref, w_ref, pad_ref):
    rows = x_ref.shape[0]
    pad_ref[pl.ds(8, rows), :] = x_ref[...].astype(f32)
    pad_ref[6:8, :] = rim_ref[...]
    return (
        w_ref[0:1] * pad_ref[pl.ds(6, rows), :]
        + w_ref[1:2] * pad_ref[pl.ds(7, rows), :]
        + w_ref[2:3] * pad_ref[pl.ds(8, rows), :]
    ).astype(bf16)


def state_kernel(start_ref, k_ref, v_ref, rk_ref, rv_ref, ck_ref, cv_ref, *refs):
    kc_ref, vc_ref, kv_ref, kpad, vpad = refs[-5:]
    kc = conv(k_ref, rk_ref, ck_ref, kpad)
    kc_ref[...] = kc
    vc_ref[...] = conv(v_ref, rv_ref, cv_ref, vpad)
    kt = (kc.astype(f32) * 0.5).T
    rows = kt.shape[1]
    place = lax.broadcasted_iota(jnp.int32, (FEAT, rows), 0)
    for h in range(GROUP):
        a = kt[FEAT * h : FEAT * (h + 1)]
        parts = [a, a * a] + [a * pltpu.roll(a, d, 0) for d in range(1, 8)]
        last = jnp.where(place >= 8, a * pltpu.roll(a, 8, 0), jnp.where(place == 0, 1.0, 0.0))
        feats = jnp.concatenate([p.astype(bf16) for p in parts + [last]], axis=0)
        kv_ref[h] = jnp.dot(
            feats, vc_ref[:, HD * h : HD * (h + 1)], preferred_element_type=f32
        ).astype(bf16)


def local_kernel(q_ref, rq_ref, cq_ref, kc_ref, vc_ref, *refs):
    qc_ref, loc_ref, qpad = refs[-3:]
    qc = conv(q_ref, rq_ref, cq_ref, qpad)
    qc_ref[...] = qc
    rows = qc.shape[0]
    half = rows // 2
    head_of = lax.broadcasted_iota(jnp.int32, qc.shape, 1) // FEAT
    scaled = qc * jnp.asarray(0.25, bf16)
    keys = kc_ref[...]
    causal = lax.broadcasted_iota(jnp.int32, (half, half), 0) >= lax.broadcasted_iota(
        jnp.int32, (half, half), 1
    )
    across = (((1,), (1,)), ((), ()))

    def doubled(s):
        p = s + 1.0
        return p * p + 1.0

    for h in range(GROUP):
        own = jnp.where(head_of == h, scaled, jnp.zeros_like(scaled))
        vh = vc_ref[:, HD * h : HD * (h + 1)]
        s0 = lax.dot_general(own[:half], keys[:half], across, preferred_element_type=f32)
        s1 = lax.dot_general(own[half:], keys, across, preferred_element_type=f32)
        t0 = jnp.where(causal, doubled(s0), 0.0).astype(bf16)
        t10 = doubled(s1[:, :half]).astype(bf16)
        t11 = jnp.where(causal, doubled(s1[:, half:]), 0.0).astype(bf16)
        loc_ref[:half, HD * h : HD * (h + 1)] = 0.5 * jnp.dot(
            t0, vh[:half], preferred_element_type=f32
        )
        loc_ref[half:, HD * h : HD * (h + 1)] = 0.5 * jnp.dot(
            jnp.concatenate([t10, t11], axis=1), vh, preferred_element_type=f32
        )


def hidden_kernel(start_ref, qc_ref, loc_ref, s_ref, gain_ref, out_ref, wide):
    width = GROUP * FEAT

    @pl.when(pl.program_id(0) == 0)
    def _():
        wide[...] = jnp.zeros_like(wide)

    for h in range(GROUP):
        for d in range(STATE // FEAT):
            wide[width * d + FEAT * h : width * d + FEAT * (h + 1), HD * h : HD * (h + 1)] = s_ref[
                h, FEAT * d : FEAT * (d + 1), :
            ]
    b = qc_ref[...].astype(f32) * 0.5
    place = lax.broadcasted_iota(jnp.int32, b.shape, 1) % FEAT

    def turned(d):
        return jnp.where(place >= d, pltpu.roll(b, d, 1), pltpu.roll(b, width - FEAT + d, 1))

    parts = [b, 0.5 * b * b] + [b * turned(d) for d in range(1, 8)]
    parts.append(jnp.where(place >= 8, b * turned(8), jnp.where(place == 0, 1.0, 0.0)))
    feats = jnp.concatenate([p.astype(bf16) for p in parts], axis=1)
    for h in range(0, GROUP, 2):
        pair = slice(HD * h, HD * (h + 2))
        both = loc_ref[:, pair] + jnp.dot(feats, wide[:, pair], preferred_element_type=f32)
        for e in range(2):
            y = both[:, HD * e : HD * (e + 1)]
            cols = slice(HD * (h + e), HD * (h + e + 1))
            scale = lax.rsqrt(jnp.mean(y * y, axis=-1, keepdims=True) + 1e-05)
            out_ref[:, cols] = (y * scale * gain_ref[:, cols]).astype(bf16)


def project_kernel(pieces, own, far, skip, first_ref, place_ref, *refs):
    sides = own + far
    hidden, weights = refs[: 2 * sides], refs[2 * sides : 2 * sides + pieces]
    rows_in, held, done, hid_sems, sems, out_sems = refs[-6:]
    outs = refs[-6 - sides : -6]
    depth = hidden[0].shape[1]
    loads = []
    for p in range(2 * sides):
        turned = p + (0 if own and p < 2 else 1)
        at = pl.multiple_of((first_ref[0] + turned) % 2 * depth, depth)
        loads.append(
            pltpu.make_async_copy(
                hidden[p], rows_in.at[p // 2, :, pl.ds(at, depth)], hid_sems.at[p]
            )
        )
    copies = [
        pltpu.make_async_copy(weights[i], held.at[:, HD * i : HD * (i + 1)], sems.at[i])
        for i in range(pieces)
    ]
    near = 2 * own
    if skip:
        loads = loads[near:] + loads[:near]
        near = 2 * far
    bounds = [0, min(2, pieces)] + list(range(6, pieces, 4)) + [pieces] * (pieces > 2)
    groups = [range(c, e) for c, e in zip(bounds, bounds[1:])]
    ahead = [copies[g[0] : g[-1] + 1] for g in groups] + [[], []]
    for copy in loads[:near] + ahead[0]:
        copy.start()
    stores = []
    for at, group in enumerate(groups):
        if at == 0:
            for copy in loads[:near]:
                copy.wait()
        for copy in ahead[at]:
            copy.wait()
        for copy in (loads[near:] if at == 0 else []) + ahead[at + 1]:
            copy.start()
        cols = slice(HD * group[0], HD * (group[-1] + 1))

        def mine():
            total = jnp.dot(rows_in[0], held[:, cols], preferred_element_type=f32).astype(bf16)
            for j, i in enumerate(group):
                done[i] = total[:, HD * j : HD * (j + 1)]
                where = pl.multiple_of(place_ref[i] * HD, HD)
                store = pltpu.make_async_copy(
                    done.at[i], outs[0].at[:, pl.ds(where, HD)], out_sems.at[i]
                )
                store.start()
                stores.append(store)

        def theirs():
            total = jnp.dot(rows_in[sides - 1], held[:, cols], preferred_element_type=f32)
            for j, i in enumerate(group):
                outs[-1][i] = total[:, HD * j : HD * (j + 1)].astype(bf16)

        if skip:
            theirs()
        elif own:
            mine()
        if at == 0:
            for copy in loads[near:]:
                copy.wait()
        if skip and group[0] >= skip:
            mine()
        elif far and not skip:
            theirs()
    for store in stores:
        store.wait()


def project(own, far, first, width, pieces, places, before=(), skip=0, micros=5):
    rows, half = (own + far)[0].shape
    count, depth = len(pieces), pieces[0].shape[0]
    smem, vmem, anywhere = (pl.BlockSpec(memory_space=m) for m in (pltpu.SMEM, pltpu.VMEM, pl.ANY))
    sides = [bool(own), bool(far)]
    outs = [
        (anywhere, jax.ShapeDtypeStruct((rows, width), bf16)),
        (vmem, jax.ShapeDtypeStruct((count, rows, HD), bf16)),
    ]
    outs = [o for o, wanted in zip(outs, sides) if wanted]
    return pl.pallas_call(
        functools.partial(project_kernel, count, *sides, skip),
        in_specs=[smem] * 2 + [anywhere] * (2 * sum(sides) + count + len(before)),
        out_specs=[o[0] for o in outs],
        out_shape=[o[1] for o in outs],
        scratch_shapes=[
            pltpu.VMEM((sum(sides), rows, 2 * half), bf16),
            pltpu.VMEM((depth, HD * count), bf16),
            pltpu.VMEM((count, rows, HD), bf16),
            pltpu.SemaphoreType.DMA((4,)),
            pltpu.SemaphoreType.DMA((count,)),
            pltpu.SemaphoreType.DMA((count,)),
        ],
        input_output_aliases={2 + 2 * sum(sides) + count: 0} if before else {},
        compiler_params=pltpu.CompilerParams(vmem_limit_bytes=VMEM),
        cost_estimate=cost(micros),
    )(first, places, *own, *far, *pieces, *before)


def beat_kernel(in_ref, out_ref):
    for i in range(in_ref.shape[0]):
        out_ref[i] = in_ref[i]


def beat(x):
    smem = pl.BlockSpec(memory_space=pltpu.SMEM)
    return pl.pallas_call(
        beat_kernel,
        in_specs=[smem],
        out_specs=smem,
        out_shape=jax.ShapeDtypeStruct(x.shape, x.dtype),
        cost_estimate=cost(5),
    )(x)


def place_kernel(counts, place_ref, *refs):
    blocks, out_ref, sems = refs[: len(counts)], refs[-2], refs[-1]
    copies = []
    for ref, count in zip(blocks, counts):
        for i in range(count):
            at = len(copies)
            where = pl.multiple_of(place_ref[at] * HD, HD)
            copy = pltpu.make_async_copy(ref.at[i], out_ref.at[:, pl.ds(where, HD)], sems.at[at])
            copy.start()
            copies.append(copy)
    for copy in copies:
        copy.wait()


def place(blocks, places, out):
    counts = [b.shape[0] for b in blocks]
    smem, vmem, anywhere = (pl.BlockSpec(memory_space=m) for m in (pltpu.SMEM, pltpu.VMEM, pl.ANY))
    return pl.pallas_call(
        functools.partial(place_kernel, counts),
        in_specs=[smem] + [vmem] * len(blocks) + [anywhere],
        out_specs=anywhere,
        out_shape=jax.ShapeDtypeStruct(out.shape, bf16),
        scratch_shapes=[pltpu.SemaphoreType.DMA((sum(counts),))],
        input_output_aliases={1 + len(blocks): 0},
        compiler_params=pltpu.CompilerParams(vmem_limit_bytes=VMEM),
        cost_estimate=cost(3),
    )(places, *blocks, out)


def ring(n):
    order = list(range(n))
    return order[:1] + order[1::2] + order[2::2][::-1]


def turn(x, axis):
    order = ring(lax.axis_size(axis) // 8)
    route = []
    for at, plane in enumerate(order):
        onto = order[(at + 1) % len(order)]
        route += [(plane * 8 + i, onto * 8 + i) for i in range(8)]
    return lax.ppermute(x, axis, route)


def flip(x, axis, bit):
    return lax.ppermute(x, axis, [(i, i ^ bit) for i in range(lax.axis_size(axis))])


def after(x, axis, distance):
    n = lax.axis_size(axis)
    return lax.ppermute(x, axis, [(i, i + distance) for i in range(n - distance)])


def rotate(x, axis, distance):
    n = lax.axis_size(axis)
    return lax.ppermute(x, axis, [(i, (i + distance) % n) for i in range(n)])


def tie(x, *others):
    return lax.optimization_barrier((x, *others))[0]


def cost(micros):
    return pl.CostEstimate(flops=int(micros * 2 * 10**10), bytes_accessed=2**20, transcendentals=0)


def params():
    return pltpu.CompilerParams(dimension_semantics=("arbitrary",), vmem_limit_bytes=VMEM)


class Scan:
    def __init__(self, ids, axis):
        self.ids, self.axis = ids, axis
        self.n, self.me = lax.axis_size(axis), lax.axis_index(axis)
        self.core = self.me % 2
        self.first = self.me - self.core
        self.plane = self.me - self.me % 8
        self.sums = 0.0

    def eq(self, i, j):
        return (self.ids[i] == self.ids[j]).astype(f32)

    def chip(self, mine, got):
        self.kv0 = jnp.where(self.core == 0, mine, got)
        kv1 = jnp.where(self.core == 0, got, mine)
        self.joined = self.eq(self.first, self.first + 1)
        self.total = (kv1.astype(f32) + self.joined * self.kv0.astype(f32)).astype(bf16)

    def hop(self, bit):
        return flip(self.total, self.axis, bit)

    def merge(self, bit, got):
        upper = (self.me // bit) % 2
        base = self.me - self.me % (2 * bit)
        lower_last, upper_last = base + bit - 1, base + 2 * bit - 1
        link = self.eq(lower_last, upper_last)
        got = got.astype(f32)
        self.sums = self.sums + upper * self.eq(lower_last, self.first) * got
        self.total = (
            jnp.where(upper == 1, 1.0, link) * self.total.astype(f32)
            + jnp.where(upper == 1, link, 1.0) * got
        ).astype(bf16)

    def climbs(self):
        return -(-(self.n // 2 - 1) // 8)

    def cut(self):
        part = self.total.shape[0] // 4
        spot = self.me // 2 % 4
        self.total = lax.dynamic_slice_in_dim(self.total, spot * part, part, 0)
        self.below = 0.0

    def climb(self, step):
        got = rotate(self.total, self.axis, 8 * (step + 1))
        source = self.plane - 8 * step - 1
        same = (source >= 0) * self.eq(jnp.maximum(source, 0), self.plane)
        self.below = self.below + same * got.astype(f32)

    def gather_hop(self, bit):
        self.below = self.below.astype(bf16)
        return flip(self.below, self.axis, bit)

    def gather(self, bit, got):
        below = self.below
        upper = (self.me // bit) % 2 == 1
        self.below = jnp.concatenate(
            [jnp.where(upper, got, below), jnp.where(upper, below, got)], axis=0
        )

    def finish(self):
        s0 = self.sums + self.eq(self.plane, self.first) * self.below.astype(f32)
        s1 = self.joined * (s0 + self.kv0.astype(f32))
        keep = jnp.where(self.core == 0, s0, s1).astype(bf16)
        send = jnp.where(self.core == 0, s1, s0).astype(bf16)
        return keep, flip(send, self.axis, 1)


def padded(x, width):
    return x if x.shape[-1] == width else jnp.pad(x, ((0, 0), (0, width - x.shape[-1])))


def state_call(start, groups, k, v, rim, ck, cv, before=()):
    rows, heads = v.shape[0], v.shape[1] // HD
    fw, vw = GROUP * FEAT, GROUP * HD

    def cols(n, wide, offset=0):
        return pl.BlockSpec((n, wide), lambda g, s: (0, offset + s[0] + g))

    return pl.pallas_call(
        state_kernel,
        grid_spec=pltpu.PrefetchScalarGridSpec(
            num_scalar_prefetch=1,
            grid=(groups,),
            in_specs=[
                cols(rows, fw),
                cols(rows, vw),
                cols(2, fw, heads + heads // GROUP),
                cols(2, vw),
                cols(3, fw),
                cols(3, vw),
            ]
            + [pl.BlockSpec(memory_space=pl.ANY)] * len(before),
            out_specs=[
                cols(rows, fw),
                cols(rows, vw),
                pl.BlockSpec((GROUP, STATE, HD), lambda g, s: (g, 0, 0)),
            ],
            scratch_shapes=[pltpu.VMEM((rows + 8, fw), f32), pltpu.VMEM((rows + 8, vw), f32)],
        ),
        out_shape=[
            jax.ShapeDtypeStruct((rows, heads * FEAT), bf16),
            jax.ShapeDtypeStruct((rows, heads * HD), bf16),
            jax.ShapeDtypeStruct((groups * GROUP, STATE, HD), bf16),
        ],
        input_output_aliases={7 + i: i for i in range(len(before))},
        compiler_params=params(),
        cost_estimate=cost(3 * groups),
    )(start, k, v, rim, rim, ck, cv, *before)


def local_call(q, rim, cq, kc, vc, start, groups, before=()):
    rows, heads = vc.shape[0], vc.shape[1] // HD
    fw, vw = GROUP * FEAT, GROUP * HD

    def cols(n, wide, offset=0):
        return pl.BlockSpec((n, wide), lambda g: (0, offset + g))

    return pl.pallas_call(
        local_kernel,
        grid=(groups,),
        in_specs=[
            cols(rows, fw, start),
            cols(2, fw, heads + start),
            cols(3, fw, start),
            cols(rows, fw, start),
            cols(rows, vw, start),
        ]
        + [pl.BlockSpec(memory_space=pl.ANY)] * len(before),
        out_specs=[cols(rows, fw, start), cols(rows, vw, start)],
        out_shape=[
            jax.ShapeDtypeStruct((rows, heads * FEAT), bf16),
            jax.ShapeDtypeStruct((rows, heads * HD), f32),
        ],
        scratch_shapes=[pltpu.VMEM((rows + 8, fw), f32)],
        input_output_aliases={5 + i: i for i in range(len(before))},
        compiler_params=params(),
        cost_estimate=cost(3 * groups),
    )(q, rim, cq, kc, vc, *before)


def hidden_call(start, qc, local, state, gain, micros=5):
    rows, fw, vw = qc.shape[0], GROUP * FEAT, GROUP * HD
    groups = state.shape[0] // GROUP

    def cols(n, wide):
        return pl.BlockSpec((n, wide), lambda g, s: (0, s[0] + g))

    return pl.pallas_call(
        hidden_kernel,
        grid_spec=pltpu.PrefetchScalarGridSpec(
            num_scalar_prefetch=1,
            grid=(groups,),
            in_specs=[
                cols(rows, fw),
                cols(rows, vw),
                pl.BlockSpec((GROUP, STATE, HD), lambda g, s: (g, 0, 0)),
                cols(1, vw),
            ],
            out_specs=pl.BlockSpec((rows, vw), lambda g, s: (0, g)),
            scratch_shapes=[pltpu.VMEM((STATE * GROUP, vw), bf16)],
        ),
        out_shape=jax.ShapeDtypeStruct((rows, groups * vw), bf16),
        compiler_params=params(),
        cost_estimate=cost(micros),
    )(start, qc, local, state, gain)


def by_gather(q, k, v, cq, ck, cv, gain, rim, weight, ids, width):
    weight = lax.all_gather(weight, "seq", axis=1, tiled=True)
    groups = v.shape[1] // (GROUP * HD)
    zero = jnp.zeros((1,), jnp.int32)
    kc, vc, kv = state_call(zero, groups, k, v, rim, ck, cv)
    qc, local = local_call(q, rim, cq, kc, vc, 0, groups)
    scan = Scan(ids, "seq")
    half = kv.shape[0] // 2
    mine = lax.dynamic_slice_in_dim(kv, scan.core * half, half, 0)
    theirs = lax.dynamic_slice_in_dim(kv, (1 - scan.core) * half, half, 0)
    scan.chip(mine, flip(theirs, "seq", 1))
    for bit in (2, 4):
        scan.merge(bit, scan.hop(bit))
    scan.cut()
    for step in range(scan.climbs()):
        scan.climb(step)
    for bit in (2, 4):
        scan.gather(bit, scan.gather_hop(bit))
    keep, got = scan.finish()
    low = jnp.where(scan.core == 0, keep, got)
    high = jnp.where(scan.core == 0, got, keep)
    state = jnp.concatenate([low, high], axis=0)
    hidden = hidden_call(zero, qc, local, state, gain)
    return jnp.dot(hidden[:, :width], weight, preferred_element_type=f32).astype(bf16)


def by_tree(q, k, v, cq, ck, cv, gain, rim, weight, ids):
    axis = "seq"
    n, me = lax.axis_size(axis), lax.axis_index(axis)
    core = jnp.reshape(me % 2, (1,)).astype(jnp.int32)
    half = v.shape[1] // (GROUP * HD) // 2
    ties = lax.optimization_barrier

    def over_x(piece):
        return flip(piece, axis, 2)

    def over_y(piece):
        return flip(piece, axis, 4)

    def over_z(piece):
        return turn(piece, axis)

    def share(piece):
        return flip(piece, axis, 1)

    own0, width = weight, n * weight.shape[1]
    mid = weight.shape[0] // 2
    scan = Scan(ids, axis)
    *kept, theirs = state_call((1 - core) * half, half, k, v, rim, ck, cv)
    got = share(theirs)
    x0, y0, own1 = over_x(own0), over_y(own0), over_z(own0)
    kc, vc, mine = state_call(core * half, half, k, v, rim, ck, cv, kept)
    got = tie(got, mine)
    scan.chip(mine, got)
    hop_x = scan.hop(2)
    before = local_call(tie(q, scan.total), rim, cq, kc, vc, 0, half)
    y0, own1 = ties((y0, own1, before[1]))[:2]

    own2, d0 = over_z(own1), over_x(y0)
    own1u, own1l = own1[:mid], own1[mid:]
    hop_x, x0, own1u, own1l = ties((hop_x, x0, own1u, own1l, before[1]))[:4]
    scan.merge(2, hop_x)
    hop_y = scan.hop(4)
    qc, local = local_call(tie(q, scan.total), rim, cq, kc, vc, half, half, before)
    y1, x1u = over_y(tie(own1, local)), over_x(tie(own1u, local))
    hop_y, own2 = ties((hop_y, own2, local))[:2]
    scan.merge(4, hop_y)
    scan.cut()

    for step in range(scan.climbs()):
        scan.climb(step)
    scan.below, d0 = ties((scan.below, d0))
    own3 = over_z(tie(own2, scan.below))
    hop_x = scan.gather_hop(2)
    hop_x, y1, x1u = ties((hop_x, y1, x1u))
    x1l = over_x(tie(own1l, hop_x))
    x2 = over_x(tie(own2, hop_x))
    scan.gather(2, hop_x)
    hop_y = scan.gather_hop(4)
    y2 = over_y(tie(own2, hop_y))
    d1 = over_z(tie(d0, hop_y))
    scan.gather(4, hop_y)
    keep, got = scan.finish()
    keep, own3 = ties((keep, own3))
    hid_a = hidden_call(core * half, qc, local, keep, gain)
    got, x1l = ties((got, x1l, hid_a))[:2]
    x1 = jnp.concatenate([x1u, x1l], axis=0)
    x3, y3 = over_x(tie(own3, got)), over_y(tie(own3, got))
    far_a = share(hid_a)
    hid_b = hidden_call((1 - core) * half, qc, local, got, gain, 0.02)
    y2, d1, x2 = ties((y2, d1, x2, hid_b))[:3]
    d2 = over_z(d1)
    far_b = share(hid_b)
    where = [
        (0, 0), (1, 0), (2, 0), (3, 0), (0, 4), (1, 4), (2, 4), (0, 2), (1, 2), (2, 2),
        (0, 6), (1, 6), (3, 2), (3, 4), (2, 6), (3, 6),
    ]
    order = ring(n // 8)
    home = jnp.asarray(order, jnp.int32)
    spot = jnp.asarray([order.index(p) for p in range(n // 8)], jnp.int32)[me // 8]
    shift = jnp.asarray([p[0] for p in where], jnp.int32)
    bits = jnp.asarray([p[1] for p in where], jnp.int32)
    places = (home[(spot - shift) % (n // 8)] * 8 + (me % 8 ^ bits)).astype(jnp.int32)
    mark = beat(tie(places, hid_b))
    far_a, far_b, mark = ties((far_a, far_b, mark))
    own, far = (hid_a, hid_b), (far_a, far_b)
    pieces = [own0, own1, own2, own3, y0, y1, y2, x0, x1, x2, d0, d1]
    out, back_a = project(own, far, core, width, pieces, mark[:12])
    x3, y3, d2, out = ties((x3, y3, d2, out))
    d3y, d3z = over_y(x3[:mid]), over_z(d2[mid:])
    d3 = jnp.concatenate([d3y, d3z], axis=0)
    out, back_c = project(own, far, core, width, [x3, y3, d2, d3], places[12:], (out,))
    backs = [share(b) for b in (back_a, back_c)]
    return place(backs, places ^ 1, out)


def on_device(
    query_feat,
    key_feat,
    values,
    conv_query,
    conv_key,
    conv_value,
    norm_gain,
    out_weight,
    stream_ids,
):
    width = values.shape[1]
    heads = -(-width // (HD * GROUP)) * GROUP
    me = lax.axis_index("seq")
    start = jnp.logical_or(me == 0, stream_ids[me] != stream_ids[jnp.maximum(me - 1, 0)])
    keep = 1.0 - start.astype(f32)
    q, k = padded(query_feat, heads * FEAT), padded(key_feat, heads * FEAT)
    v = padded(values, heads * HD)
    cq, ck = padded(conv_query, heads * FEAT), padded(conv_key, heads * FEAT)
    cv = padded(conv_value, heads * HD)
    gain = padded(norm_gain[None], heads * HD)
    rim = after(jnp.concatenate([v[-2:], q[-2:], k[-2:]], axis=1), "seq", 1).astype(f32) * keep
    n, cut = lax.axis_size("seq"), lax.axis_size("head")
    if n == 32 and cut == 1 and out_weight.shape[1] == HD and heads % (2 * GROUP) == 0:
        return by_tree(q, k, v, cq, ck, cv, gain, rim, out_weight, stream_ids)
    terms = by_gather(q, k, v, cq, ck, cv, gain, rim, out_weight, stream_ids, width)
    return lax.psum_scatter(terms, "head", scatter_dimension=1, tiled=True)


def solution(mesh):
    placed = (
        P("seq", "head"),
        P("seq", "head"),
        P("seq", "head"),
        P(None, "head"),
        P(None, "head"),
        P(None, "head"),
        P("head"),
        P("head", "seq"),
        P(),
    )
    return jax.shard_map(
        on_device, mesh=mesh, in_specs=placed, out_specs=P("seq", "head"), check_vma=False
    )
```

```python
import functools

import jax
import jax.numpy as jnp
from jax import lax
from jax.experimental import pallas as pl
from jax.experimental.pallas import tpu as pltpu
from jax.sharding import PartitionSpec as P

HD = 128
FEAT = 16
GROUP = 8
STATE = 160
BLOCK = 512
VMEM = 56 * 2**20

f32 = jnp.float32
bf16 = jnp.bfloat16


def conv(x_ref, rim_ref, w_ref, pad_ref):
    rows = x_ref.shape[0]
    pad_ref[pl.ds(8, rows), :] = x_ref[...].astype(f32)
    pad_ref[6:8, :] = rim_ref[...]
    return (
        w_ref[0:1] * pad_ref[pl.ds(6, rows), :]
        + w_ref[1:2] * pad_ref[pl.ds(7, rows), :]
        + w_ref[2:3] * pad_ref[pl.ds(8, rows), :]
    ).astype(bf16)


def state_kernel(start_ref, k_ref, v_ref, rk_ref, rv_ref, ck_ref, cv_ref, *refs):
    kc_ref, vc_ref, kv_ref, kpad, vpad = refs[-5:]
    kc = conv(k_ref, rk_ref, ck_ref, kpad)
    kc_ref[...] = kc
    vc_ref[...] = conv(v_ref, rv_ref, cv_ref, vpad)
    kt = (kc.astype(f32) * 0.5).T
    rows = kt.shape[1]
    place = lax.broadcasted_iota(jnp.int32, (FEAT, rows), 0)
    for h in range(GROUP):
        a = kt[FEAT * h : FEAT * (h + 1)]
        parts = [a, a * a] + [a * pltpu.roll(a, d, 0) for d in range(1, 8)]
        last = jnp.where(place >= 8, a * pltpu.roll(a, 8, 0), jnp.where(place == 0, 1.0, 0.0))
        feats = jnp.concatenate([p.astype(bf16) for p in parts + [last]], axis=0)
        kv_ref[h] = jnp.dot(
            feats, vc_ref[:, HD * h : HD * (h + 1)], preferred_element_type=f32
        ).astype(bf16)


def local_kernel(q_ref, rq_ref, cq_ref, kc_ref, vc_ref, *refs):
    qc_ref, loc_ref, qpad = refs[-3:]
    qc = conv(q_ref, rq_ref, cq_ref, qpad)
    qc_ref[...] = qc
    rows = qc.shape[0]
    half = rows // 2
    head_of = lax.broadcasted_iota(jnp.int32, qc.shape, 1) // FEAT
    scaled = qc * jnp.asarray(0.25, bf16)
    keys = kc_ref[...]
    causal = lax.broadcasted_iota(jnp.int32, (half, half), 0) >= lax.broadcasted_iota(
        jnp.int32, (half, half), 1
    )
    across = (((1,), (1,)), ((), ()))

    def doubled(s):
        p = s + 1.0
        return p * p + 1.0

    for h in range(GROUP):
        own = jnp.where(head_of == h, scaled, jnp.zeros_like(scaled))
        vh = vc_ref[:, HD * h : HD * (h + 1)]
        s0 = lax.dot_general(own[:half], keys[:half], across, preferred_element_type=f32)
        s1 = lax.dot_general(own[half:], keys, across, preferred_element_type=f32)
        t0 = jnp.where(causal, doubled(s0), 0.0).astype(bf16)
        t10 = doubled(s1[:, :half]).astype(bf16)
        t11 = jnp.where(causal, doubled(s1[:, half:]), 0.0).astype(bf16)
        loc_ref[:half, HD * h : HD * (h + 1)] = 0.5 * jnp.dot(
            t0, vh[:half], preferred_element_type=f32
        )
        loc_ref[half:, HD * h : HD * (h + 1)] = 0.5 * jnp.dot(
            jnp.concatenate([t10, t11], axis=1), vh, preferred_element_type=f32
        )


def hidden_kernel(start_ref, qc_ref, loc_ref, s_ref, gain_ref, out_ref, wide):
    width = GROUP * FEAT

    @pl.when(pl.program_id(0) == 0)
    def _():
        wide[...] = jnp.zeros_like(wide)

    for h in range(GROUP):
        for d in range(STATE // FEAT):
            wide[width * d + FEAT * h : width * d + FEAT * (h + 1), HD * h : HD * (h + 1)] = s_ref[
                h, FEAT * d : FEAT * (d + 1), :
            ]
    b = qc_ref[...].astype(f32) * 0.5
    place = lax.broadcasted_iota(jnp.int32, b.shape, 1) % FEAT

    def turned(d):
        return jnp.where(place >= d, pltpu.roll(b, d, 1), pltpu.roll(b, width - FEAT + d, 1))

    parts = [b, 0.5 * b * b] + [b * turned(d) for d in range(1, 8)]
    parts.append(jnp.where(place >= 8, b * turned(8), jnp.where(place == 0, 1.0, 0.0)))
    feats = jnp.concatenate([p.astype(bf16) for p in parts], axis=1)
    for h in range(0, GROUP, 2):
        pair = slice(HD * h, HD * (h + 2))
        both = loc_ref[:, pair] + jnp.dot(feats, wide[:, pair], preferred_element_type=f32)
        for e in range(2):
            y = both[:, HD * e : HD * (e + 1)]
            cols = slice(HD * (h + e), HD * (h + e + 1))
            scale = lax.rsqrt(jnp.mean(y * y, axis=-1, keepdims=True) + 1e-05)
            out_ref[:, cols] = (y * scale * gain_ref[:, cols]).astype(bf16)


def project_kernel(parts, own, far, first_ref, place_ref, *refs):
    sides, pieces = own + far, len(parts)
    hidden, weights = refs[: 2 * sides], list(refs[2 * sides :])
    rows_in, held, done, hid_sems, sems, out_sems = refs[-6:]
    outs = refs[-6 - sides : -6]
    depth = hidden[0].shape[1]
    loads = []
    for p in range(2 * sides):
        turned = p + (0 if own and p < 2 else 1)
        at = pl.multiple_of((first_ref[0] + turned) % 2 * depth, depth)
        loads.append(
            pltpu.make_async_copy(
                hidden[p], rows_in.at[p // 2, :, pl.ds(at, depth)], hid_sems.at[p]
            )
        )
    copies = []
    for i in range(pieces):
        row, copies_of = 0, []
        for _ in range(parts[i]):
            ref = weights.pop(0)
            to = held.at[row : row + ref.shape[0], HD * i : HD * (i + 1)]
            copies_of.append(pltpu.make_async_copy(ref, to, sems.at[i, len(copies_of)]))
            row += ref.shape[0]
        copies.append(copies_of)
    near = 2 * own
    bounds = [0, min(2, pieces)] + list(range(6, pieces, 4)) + [pieces] * (pieces > 2)
    groups = [range(c, e) for c, e in zip(bounds, bounds[1:])]
    ahead = [[c for i in g for c in copies[i]] for g in groups] + [[]]
    for copy in loads[:near] + ahead[0]:
        copy.start()
    stores = []
    for at, group in enumerate(groups):
        if at == 0:
            for copy in loads[:near]:
                copy.wait()
        for copy in ahead[at]:
            copy.wait()
        for copy in (loads[near:] if at == 0 else []) + ahead[at + 1]:
            copy.start()
        cols = slice(HD * group[0], HD * (group[-1] + 1))

        def mine():
            total = jnp.dot(rows_in[0], held[:, cols], preferred_element_type=f32).astype(bf16)
            for j, i in enumerate(group):
                done[i] = total[:, HD * j : HD * (j + 1)]
                where = pl.multiple_of(place_ref[i] * HD, HD)
                store = pltpu.make_async_copy(
                    done.at[i], outs[0].at[:, pl.ds(where, HD)], out_sems.at[i]
                )
                store.start()
                stores.append(store)

        def theirs():
            total = jnp.dot(rows_in[sides - 1], held[:, cols], preferred_element_type=f32)
            for j, i in enumerate(group):
                outs[-1][i] = total[:, HD * j : HD * (j + 1)].astype(bf16)

        if own:
            mine()
        if at == 0:
            for copy in loads[near:]:
                copy.wait()
        if far:
            theirs()
    for store in stores:
        store.wait()


def project(own, far, first, width, pieces, places, before=()):
    rows, half = (own + far)[0].shape
    pieces = [p if isinstance(p, tuple) else (p,) for p in pieces]
    count, depth, parts = len(pieces), 2 * half, [len(p) for p in pieces]
    smem, vmem, anywhere = (pl.BlockSpec(memory_space=m) for m in (pltpu.SMEM, pltpu.VMEM, pl.ANY))
    sides = [bool(own), bool(far)]
    outs = [
        (anywhere, jax.ShapeDtypeStruct((rows, width), bf16)),
        (vmem, jax.ShapeDtypeStruct((count, rows, HD), bf16)),
    ]
    outs = [o for o, wanted in zip(outs, sides) if wanted]
    return pl.pallas_call(
        functools.partial(project_kernel, parts, *sides),
        in_specs=[smem] * 2 + [anywhere] * (2 * sum(sides) + sum(parts) + len(before)),
        out_specs=[o[0] for o in outs],
        out_shape=[o[1] for o in outs],
        scratch_shapes=[
            pltpu.VMEM((sum(sides), rows, 2 * half), bf16),
            pltpu.VMEM((depth, HD * count), bf16),
            pltpu.VMEM((count, rows, HD), bf16),
            pltpu.SemaphoreType.DMA((4,)),
            pltpu.SemaphoreType.DMA((count, max(parts))),
            pltpu.SemaphoreType.DMA((count,)),
        ],
        input_output_aliases={2 + 2 * sum(sides) + sum(parts): 0} if before else {},
        compiler_params=pltpu.CompilerParams(vmem_limit_bytes=VMEM),
        cost_estimate=cost(5),
    )(first, places, *own, *far, *(a for p in pieces for a in p), *before)


def beat_kernel(in_ref, out_ref):
    for i in range(in_ref.shape[0]):
        out_ref[i] = in_ref[i]


def beat(x):
    smem = pl.BlockSpec(memory_space=pltpu.SMEM)
    return pl.pallas_call(
        beat_kernel,
        in_specs=[smem],
        out_specs=smem,
        out_shape=jax.ShapeDtypeStruct(x.shape, x.dtype),
        cost_estimate=cost(5),
    )(x)


def place_kernel(counts, place_ref, *refs):
    blocks, out_ref, sems = refs[: len(counts)], refs[-2], refs[-1]
    copies = []
    for ref, count in zip(blocks, counts):
        for i in range(count):
            at = len(copies)
            where = pl.multiple_of(place_ref[at] * HD, HD)
            copy = pltpu.make_async_copy(ref.at[i], out_ref.at[:, pl.ds(where, HD)], sems.at[at])
            copy.start()
            copies.append(copy)
    for copy in copies:
        copy.wait()


def place(blocks, places, out):
    counts = [b.shape[0] for b in blocks]
    smem, vmem, anywhere = (pl.BlockSpec(memory_space=m) for m in (pltpu.SMEM, pltpu.VMEM, pl.ANY))
    return pl.pallas_call(
        functools.partial(place_kernel, counts),
        in_specs=[smem] + [vmem] * len(blocks) + [anywhere],
        out_specs=anywhere,
        out_shape=jax.ShapeDtypeStruct(out.shape, bf16),
        scratch_shapes=[pltpu.SemaphoreType.DMA((sum(counts),))],
        input_output_aliases={1 + len(blocks): 0},
        compiler_params=pltpu.CompilerParams(vmem_limit_bytes=VMEM),
        cost_estimate=cost(3),
    )(places, *blocks, out)


def ring(n):
    order = list(range(n))
    return order[:1] + order[1::2] + order[2::2][::-1]


def turn(x, axis):
    order = ring(lax.axis_size(axis) // 8)
    route = []
    for at, plane in enumerate(order):
        onto = order[(at + 1) % len(order)]
        route += [(plane * 8 + i, onto * 8 + i) for i in range(8)]
    return lax.ppermute(x, axis, route)


def flip(x, axis, bit):
    return lax.ppermute(x, axis, [(i, i ^ bit) for i in range(lax.axis_size(axis))])


def after(x, axis, distance):
    n = lax.axis_size(axis)
    return lax.ppermute(x, axis, [(i, i + distance) for i in range(n - distance)])


def rotate(x, axis, distance):
    n = lax.axis_size(axis)
    return lax.ppermute(x, axis, [(i, (i + distance) % n) for i in range(n)])


def tie(x, *others):
    return lax.optimization_barrier((x, *others))[0]


def cost(micros):
    return pl.CostEstimate(flops=int(micros * 2 * 10**10), bytes_accessed=2**20, transcendentals=0)


def params():
    return pltpu.CompilerParams(dimension_semantics=("arbitrary",), vmem_limit_bytes=VMEM)


def pick(ids, i):
    return ids.at[i].get(mode="promise_in_bounds", wrap_negative_indices=False)


class Scan:
    def __init__(self, ids, axis):
        self.ids, self.axis = ids, axis
        self.n, self.me = lax.axis_size(axis), lax.axis_index(axis)
        self.core = self.me & 1
        self.first = self.me - self.core
        self.plane = self.me & ~7
        self.sums = 0.0

    def eq(self, i, j):
        return (pick(self.ids, i) == pick(self.ids, j)).astype(f32)

    def chip(self, mine, got):
        self.kv0 = jnp.where(self.core == 0, mine, got)
        kv1 = jnp.where(self.core == 0, got, mine)
        self.joined = self.eq(self.first, self.first + 1)
        self.total = (kv1.astype(f32) + self.joined * self.kv0.astype(f32)).astype(bf16)

    def hop(self, bit):
        return flip(self.total, self.axis, bit)

    def merge(self, bit, got):
        upper = lax.shift_right_logical(self.me & bit, bit // 2)
        base = self.me & ~(2 * bit - 1)
        lower_last, upper_last = base + bit - 1, base + 2 * bit - 1
        link = self.eq(lower_last, upper_last)
        got = got.astype(f32)
        self.sums = self.sums + upper * self.eq(lower_last, self.first) * got
        self.total = (
            jnp.where(upper == 1, 1.0, link) * self.total.astype(f32)
            + jnp.where(upper == 1, link, 1.0) * got
        ).astype(bf16)

    def climbs(self):
        return -(-(self.n // 2 - 1) // 8)

    def cut(self):
        part = self.total.shape[0] // 4
        spot = lax.shift_right_logical(self.me & 6, 1)
        self.total = lax.dynamic_slice_in_dim(self.total, spot * part, part, 0)
        self.below = 0.0

    def climb(self, step):
        got = rotate(self.total, self.axis, 8 * (step + 1))
        source = self.plane - 8 * step - 1
        same = (source >= 0) * self.eq(jnp.maximum(source, 0), self.plane)
        self.below = self.below + same * got.astype(f32)

    def gather_hop(self, bit):
        self.below = self.below.astype(bf16)
        return flip(self.below, self.axis, bit)

    def gather(self, bit, got):
        below = self.below
        upper = (self.me & bit) != 0
        self.below = jnp.concatenate(
            [jnp.where(upper, got, below), jnp.where(upper, below, got)], axis=0
        )

    def finish(self):
        s0 = self.sums + self.eq(self.plane, self.first) * self.below.astype(f32)
        s1 = self.joined * (s0 + self.kv0.astype(f32))
        keep = jnp.where(self.core == 0, s0, s1).astype(bf16)
        send = jnp.where(self.core == 0, s1, s0).astype(bf16)
        return keep, flip(send, self.axis, 1)


def padded(x, width):
    return x if x.shape[-1] == width else jnp.pad(x, ((0, 0), (0, width - x.shape[-1])))


def state_call(start, groups, k, v, rim, ck, cv, before=()):
    rows, heads = v.shape[0], v.shape[1] // HD
    fw, vw = GROUP * FEAT, GROUP * HD

    def cols(n, wide, offset=0):
        return pl.BlockSpec((n, wide), lambda g, s: (0, offset + s[0] + g))

    return pl.pallas_call(
        state_kernel,
        grid_spec=pltpu.PrefetchScalarGridSpec(
            num_scalar_prefetch=1,
            grid=(groups,),
            in_specs=[
                cols(rows, fw),
                cols(rows, vw),
                cols(2, fw, heads + heads // GROUP),
                cols(2, vw),
                cols(3, fw),
                cols(3, vw),
            ]
            + [pl.BlockSpec(memory_space=pl.ANY)] * len(before),
            out_specs=[
                cols(rows, fw),
                cols(rows, vw),
                pl.BlockSpec((GROUP, STATE, HD), lambda g, s: (g, 0, 0)),
            ],
            scratch_shapes=[pltpu.VMEM((rows + 8, fw), f32), pltpu.VMEM((rows + 8, vw), f32)],
        ),
        out_shape=[
            jax.ShapeDtypeStruct((rows, heads * FEAT), bf16),
            jax.ShapeDtypeStruct((rows, heads * HD), bf16),
            jax.ShapeDtypeStruct((groups * GROUP, STATE, HD), bf16),
        ],
        input_output_aliases={7 + i: i for i in range(len(before))},
        compiler_params=params(),
        cost_estimate=cost(3 * groups),
    )(start, k, v, rim, rim, ck, cv, *before)


def local_call(q, rim, cq, kc, vc, start, groups, before=()):
    rows, heads = vc.shape[0], vc.shape[1] // HD
    fw, vw = GROUP * FEAT, GROUP * HD

    def cols(n, wide, offset=0):
        return pl.BlockSpec((n, wide), lambda g: (0, offset + g))

    return pl.pallas_call(
        local_kernel,
        grid=(groups,),
        in_specs=[
            cols(rows, fw, start),
            cols(2, fw, heads + start),
            cols(3, fw, start),
            cols(rows, fw, start),
            cols(rows, vw, start),
        ]
        + [pl.BlockSpec(memory_space=pl.ANY)] * len(before),
        out_specs=[cols(rows, fw, start), cols(rows, vw, start)],
        out_shape=[
            jax.ShapeDtypeStruct((rows, heads * FEAT), bf16),
            jax.ShapeDtypeStruct((rows, heads * HD), f32),
        ],
        scratch_shapes=[pltpu.VMEM((rows + 8, fw), f32)],
        input_output_aliases={5 + i: i for i in range(len(before))},
        compiler_params=params(),
        cost_estimate=cost(3 * groups),
    )(q, rim, cq, kc, vc, *before)


def hidden_call(start, qc, local, state, gain, micros=5):
    rows, fw, vw = qc.shape[0], GROUP * FEAT, GROUP * HD
    groups = state.shape[0] // GROUP

    def cols(n, wide):
        return pl.BlockSpec((n, wide), lambda g, s: (0, s[0] + g))

    return pl.pallas_call(
        hidden_kernel,
        grid_spec=pltpu.PrefetchScalarGridSpec(
            num_scalar_prefetch=1,
            grid=(groups,),
            in_specs=[
                cols(rows, fw),
                cols(rows, vw),
                pl.BlockSpec((GROUP, STATE, HD), lambda g, s: (g, 0, 0)),
                cols(1, vw),
            ],
            out_specs=pl.BlockSpec((rows, vw), lambda g, s: (0, g)),
            scratch_shapes=[pltpu.VMEM((STATE * GROUP, vw), bf16)],
        ),
        out_shape=jax.ShapeDtypeStruct((rows, groups * vw), bf16),
        compiler_params=params(),
        cost_estimate=cost(micros),
    )(start, qc, local, state, gain)


def by_gather(q, k, v, cq, ck, cv, gain, rim, weight, ids, width):
    weight = lax.all_gather(weight, "seq", axis=1, tiled=True)
    groups = v.shape[1] // (GROUP * HD)
    zero = jnp.zeros((1,), jnp.int32)
    kc, vc, kv = state_call(zero, groups, k, v, rim, ck, cv)
    qc, local = local_call(q, rim, cq, kc, vc, 0, groups)
    scan = Scan(ids, "seq")
    half = kv.shape[0] // 2
    mine = lax.dynamic_slice_in_dim(kv, scan.core * half, half, 0)
    theirs = lax.dynamic_slice_in_dim(kv, (1 - scan.core) * half, half, 0)
    scan.chip(mine, flip(theirs, "seq", 1))
    for bit in (2, 4):
        scan.merge(bit, scan.hop(bit))
    scan.cut()
    for step in range(scan.climbs()):
        scan.climb(step)
    for bit in (2, 4):
        scan.gather(bit, scan.gather_hop(bit))
    keep, got = scan.finish()
    low = jnp.where(scan.core == 0, keep, got)
    high = jnp.where(scan.core == 0, got, keep)
    state = jnp.concatenate([low, high], axis=0)
    hidden = hidden_call(zero, qc, local, state, gain)
    return jnp.dot(hidden[:, :width], weight, preferred_element_type=f32).astype(bf16)


def by_tree(q, k, v, cq, ck, cv, gain, rim, weight, ids):
    axis = "seq"
    n, me = lax.axis_size(axis), lax.axis_index(axis)
    core = jnp.reshape(me & 1, (1,)).astype(jnp.int32)
    half = v.shape[1] // (GROUP * HD) // 2
    ties = lax.optimization_barrier

    def over_x(piece):
        return flip(piece, axis, 2)

    def over_y(piece):
        return flip(piece, axis, 4)

    def over_z(piece):
        return turn(piece, axis)

    def share(piece):
        return flip(piece, axis, 1)

    own0, width = weight, n * weight.shape[1]
    mid = weight.shape[0] // 2
    scan = Scan(ids, axis)
    *kept, theirs = state_call((1 - core) * half, half, k, v, rim, ck, cv)
    got = share(theirs)
    x0, y0, own1 = over_x(own0), over_y(own0), over_z(own0)
    kc, vc, mine = state_call(core * half, half, k, v, rim, ck, cv, kept)
    got = tie(got, mine)
    scan.chip(mine, got)
    hop_x = scan.hop(2)
    before = local_call(tie(q, scan.total), rim, cq, kc, vc, 0, half)
    y0, own1 = ties((y0, own1, before[1]))[:2]

    own2, d0 = over_z(own1), over_x(y0)
    own1u, own1l = own1[:mid], own1[mid:]
    hop_x, x0, own1u, own1l = ties((hop_x, x0, own1u, own1l, before[1]))[:4]
    scan.merge(2, hop_x)
    hop_y = scan.hop(4)
    qc, local = local_call(tie(q, scan.total), rim, cq, kc, vc, half, half, before)
    y1, x1u = over_y(tie(own1, local)), over_x(tie(own1u, local))
    hop_y, own2 = ties((hop_y, own2, local))[:2]
    scan.merge(4, hop_y)
    scan.cut()

    for step in range(scan.climbs()):
        scan.climb(step)
    mark = beat(tie(core, scan.total))
    own3 = over_z(tie(own2, mark))
    scan.below, d0, mark = ties((scan.below, d0, mark))
    hop_x = scan.gather_hop(2)
    hop_x, y1, x1u = ties((hop_x, y1, x1u))
    x1l = over_x(tie(own1l, hop_x))
    x2 = over_x(tie(own2, hop_x))
    scan.gather(2, hop_x)
    hop_y = scan.gather_hop(4)
    y2 = over_y(tie(own2, hop_y))
    d1 = over_z(tie(d0, hop_y))
    scan.gather(4, hop_y)
    keep, got = scan.finish()
    keep, own3 = ties((keep, own3))
    hid_a = hidden_call(core * half, qc, local, keep, gain)
    got, x1l = ties((got, x1l, hid_a))[:2]
    x1 = (x1u, x1l)
    x3, y3 = over_x(tie(own3, got)), over_y(tie(own3, got))
    far_a = share(hid_a)
    hid_b = hidden_call((1 - core) * half, qc, local, got, gain, 0.02)
    y2, d1, x2 = ties((y2, d1, x2, hid_b))[:3]
    d2 = over_z(d1)
    far_b = share(hid_b)
    where = [
        (0, 0), (1, 0), (2, 0), (3, 0), (0, 4), (1, 4), (0, 2), (1, 2), (0, 6), (1, 6),
        (2, 4), (2, 2), (3, 2), (3, 4), (2, 6), (3, 6),
    ]
    order = ring(n // 8)
    me = tie(me, hid_a)
    plane = lax.shift_right_logical(me, 3)
    spot = sum(jnp.where(plane == p, i, 0) for i, p in enumerate(order))
    shift = jnp.asarray([p[0] for p in where], jnp.int32)
    bits = jnp.asarray([p[1] for p in where], jnp.int32)
    turned = (spot - shift) & (n // 8 - 1)
    home = sum(jnp.where(turned == i, p, 0) for i, p in enumerate(order))
    places = (home * 8 + ((me & 7) ^ bits)).astype(jnp.int32)
    mark = beat(tie(places, hid_b))
    far_a, far_b, mark = ties((far_a, far_b, mark))
    own, far = (hid_a, hid_b), (far_a, far_b)
    pieces = [own0, own1, own2, own3, y0, y1, x0, x1, d0, d1, y2]
    out, back_a = project(own, far, core, width, pieces, mark[:11])
    x3, d2, out = ties((x3, d2, out))
    d3 = (over_y(x3[:mid]), over_z(d2[mid:]))
    y3, out = ties((y3, out))
    pieces = [x2, x3, y3]
    out, back_b = project(own, far, core, width, pieces, places[11:14], (out,))
    *d3, out = ties((*d3, out, back_b))[:3]
    out, back_c = project(own, far, core, width, [d2, tuple(d3)], places[14:], (out,))
    backs = [share(b) for b in (back_a, back_b, back_c)]
    return place(backs, places ^ 1, out)


def on_device(
    query_feat,
    key_feat,
    values,
    conv_query,
    conv_key,
    conv_value,
    norm_gain,
    out_weight,
    stream_ids,
):
    width = values.shape[1]
    heads = -(-width // (HD * GROUP)) * GROUP
    me = lax.axis_index("seq")
    start = jnp.logical_or(me == 0, pick(stream_ids, me) != pick(stream_ids, jnp.maximum(me - 1, 0)))
    keep = 1.0 - start.astype(f32)
    q, k = padded(query_feat, heads * FEAT), padded(key_feat, heads * FEAT)
    v = padded(values, heads * HD)
    cq, ck = padded(conv_query, heads * FEAT), padded(conv_key, heads * FEAT)
    cv = padded(conv_value, heads * HD)
    gain = padded(norm_gain[None], heads * HD)
    last = jnp.concatenate([v[-2:], q[-2:], k[-2:]], axis=1)
    rim = after(last, "seq", 1).astype(f32) * keep
    n, cut = lax.axis_size("seq"), lax.axis_size("head")
    if n == 32 and cut == 1 and out_weight.shape[1] == HD and heads % (2 * GROUP) == 0:
        weight = tie(out_weight, last)
        return by_tree(q, k, v, cq, ck, cv, gain, rim, weight, stream_ids)
    terms = by_gather(q, k, v, cq, ck, cv, gain, rim, out_weight, stream_ids, width)
    return lax.psum_scatter(terms, "head", scatter_dimension=1, tiled=True)


def solution(mesh):
    placed = (
        P("seq", "head"),
        P("seq", "head"),
        P("seq", "head"),
        P(None, "head"),
        P(None, "head"),
        P(None, "head"),
        P("head"),
        P("head", "seq"),
        P(),
    )
    return jax.shard_map(
        on_device, mesh=mesh, in_specs=placed, out_specs=P("seq", "head"), check_vma=False
    )
```
